32 devices in a mesh: groups: 2 (over x), adapter: 16 (over z, y, core).
Axes of the slice: x: 2, y: 2, z: 4, core: 2. Of those that a mesh axis runs over, the one named last changes fastest.
Arguments:
- tokens: bfloat16 [8192, 8192], P(('groups', 'adapter')), parts along dimension 0, may hold values from -6 to 6
- down_weight: bfloat16 [8192, 2048], P(None, 'adapter'), may hold values from -0.0625 to 0.0625
- up_weight: bfloat16 [2048, 8192], P('adapter'), may hold values from -0.75 to 0.75
- slot_adapter_index: int32 [992], P(('groups', 'adapter')), parts along dimension 0, may hold values from 0 to 31, as said below
- slot_token_length: int32 [992], P(('groups', 'adapter')), parts along dimension 0, may hold values from 0 to 48, as said below
- adapter_block_table: int32 [64], P('groups'), parts along dimension 0, may hold values from 0 to 31, as said below
Outputs:
- projection_update: bfloat16 [8192, 8192], P(('groups', 'adapter')), parts along dimension 0
The draws below stay inside these ranges and needn't reach their ends.
There are 2 independent parts, one for each index of `groups`. The reference program is written for one: setup_inputs(seed, part) draws one part's arguments, and reference() takes and returns one part's arrays. A program takes and returns all parts, laid end to end along the dimension named above; an argument that names none is the same for every part. Nothing has to cross between parts.
Inputs may be any that keep to these rules, and one draw needn't show every extreme that they name: `adapter_block_table`: A permutation: block b is stored on device b // 2 of the adapter axis. `slot_adapter_index`: slot 0 of every device uses one and the same adapter. Apart from slot 0, the slots of one device put at most 24 tokens on the adapters stored on any one device, none on the device that stores slot 0's adapter, and exactly 24 on some device. `slot_token_length`: the 31 lengths of one device sum to 256; slot 0 of each device has 48 tokens; other slots may be empty.
All inputs are finite; a program needn't handle non-finite values.
Results may differ from the reference program's by a relative error of at most 0.0051.
Values may be sent and summed in bfloat16 or wider, within the bound.
A program may use at most 128 MiB of HBM per device.

```python
import jax
import jax.numpy as jnp
from jax import lax

MODEL_WIDTH = 8192
ADAPTER_RANK = 64
TOK_DEV = 256
ADAPT_DEV = 2
ADAPTER_COUNT = 32
TOKENS = 4096
SPAN_MOST = 48
SPAN_REST = 24
REQ_DEV = 31
SPANS = 496


def shared_routing(key):
    devices = SPANS // REQ_DEV
    others_count = devices - 1
    keys = jax.random.split(key, 3)
    storage = jax.random.permutation(keys[0], ADAPTER_COUNT).astype(jnp.int32)
    holder = jnp.argsort(storage).astype(jnp.int32)
    hot = jax.random.randint(keys[1], (), 0, ADAPTER_COUNT).astype(jnp.int32)
    hot_dev = jnp.take(storage, hot) // ADAPT_DEV
    pool_size = (devices - 2) * SPAN_REST
    holes = others_count * SPAN_REST - (TOK_DEV - SPAN_MOST)
    labels = jnp.arange(pool_size, dtype=jnp.int32) // SPAN_REST
    other_ids = jnp.arange(others_count, dtype=jnp.int32)

    def one_device(dev_key):
        parts_keys = jax.random.split(dev_key, 5)
        full = jax.random.randint(parts_keys[0], (), 0, others_count).astype(jnp.int32)
        owner_of_unit = labels + (labels >= full).astype(jnp.int32)
        order = jax.random.permutation(parts_keys[1], pool_size)
        missing = jnp.take(owner_of_unit, order[:holes])
        hole_count = jnp.sum((missing[:, None] == other_ids[None, :]).astype(jnp.int32), axis=0)
        load = SPAN_REST - hole_count
        first = jax.random.randint(parts_keys[2], (others_count,), 0, load + 1).astype(jnp.int32)
        lengths_pair = jnp.stack([first, load - first], 1).reshape(-1)
        owners = other_ids + (other_ids >= hot_dev).astype(jnp.int32)
        owners_pair = jnp.repeat(owners, 2)
        slots = jax.random.randint(parts_keys[3], (2 * others_count,), 0, ADAPT_DEV).astype(jnp.int32)
        ids_pair = jnp.take(holder, owners_pair * ADAPT_DEV + slots)
        shuffle = jax.random.permutation(parts_keys[4], 2 * others_count)
        ids = jnp.concatenate([hot[None], jnp.take(ids_pair, shuffle)])
        lengths = jnp.concatenate([jnp.full((1,), SPAN_MOST, jnp.int32), jnp.take(lengths_pair, shuffle)])
        return (ids, lengths)
    ids, lengths = jax.vmap(one_device)(jax.random.split(keys[2], devices))
    return (storage, ids.reshape(-1).astype(jnp.int32), lengths.reshape(-1).astype(jnp.int32))


def draw_adapter_block_table(key, part):
    return shared_routing(key)[0]


def draw_slot_adapter_index(key, part):
    return shared_routing(key)[1]


def draw_slot_token_length(key, part):
    return shared_routing(key)[2]


def steps_of(key, shape, cuts, low, top_value):
    def one(axis_at, parts):
        draws = jax.random.uniform(jax.random.fold_in(jax.random.fold_in(key, 6), axis_at), (parts,), jnp.float32, low / len(cuts), top_value / len(cuts))
        return jnp.repeat(jnp.exp(draws), shape[axis_at] // parts).reshape((-1,) + (1,) * (len(shape) - axis_at - 1))

    loudness = one(*cuts[0])
    for cut in cuts[1:]:
        loudness = loudness * one(*cut)
    return loudness


def centred(own_key, shape, width, reach, cuts=(), held_as=jnp.bfloat16):
    array = jax.random.normal(own_key, shape, jnp.float32) * width
    if len(cuts) > 0:
        array = steps_of(own_key, shape, cuts, -0.22, 0.18) * array
    return jnp.clip(array, min=-reach, max=reach).astype(held_as)


def setup_inputs(seed: int = 0, part: int = 0) -> dict:
    seeds = jax.random.split(jax.random.key(seed), 7)
    part_keys = jax.random.split(jax.random.fold_in(seeds[6], part), 7)
    return {
        "tokens": centred(part_keys[0], (TOKENS, MODEL_WIDTH), 1.0, 6.0, ((0, 16),)),
        "down_weight": centred(seeds[1], (MODEL_WIDTH, ADAPTER_COUNT * ADAPTER_RANK), MODEL_WIDTH ** -0.5, 0.0625, ((1, 16),)),
        "up_weight": centred(seeds[2], (ADAPTER_COUNT * ADAPTER_RANK, MODEL_WIDTH), ADAPTER_RANK ** -0.5, 0.75, ((0, 16),)),
        "slot_adapter_index": draw_slot_adapter_index(jax.random.fold_in(jax.random.fold_in(seeds[6], part), 71), part),
        "slot_token_length": draw_slot_token_length(jax.random.fold_in(jax.random.fold_in(seeds[6], part), 71), part),
        "adapter_block_table": draw_adapter_block_table(jax.random.fold_in(jax.random.fold_in(seeds[6], part), 71), part),
    }


def reference(tokens, down_weight, up_weight, slot_adapter_index, slot_token_length, adapter_block_table):
    storage = jnp.take(adapter_block_table, slot_adapter_index).astype(jnp.int32)
    span_ends = jnp.cumsum(slot_token_length).astype(jnp.int32)
    span_starts = (span_ends - slot_token_length).astype(jnp.int32)
    lengths = slot_token_length.astype(jnp.int32)
    padded = jnp.concatenate([tokens, jnp.zeros((SPAN_MOST, MODEL_WIDTH), tokens.dtype)], 0)
    input_rows = jnp.transpose(down_weight).reshape(ADAPTER_COUNT, ADAPTER_RANK, MODEL_WIDTH)
    output_row_block = up_weight.reshape(ADAPTER_COUNT, ADAPTER_RANK, MODEL_WIDTH)
    offsets = jnp.arange(SPAN_MOST, dtype=jnp.int32)

    def apply_span(output_rows, span_info):
        start_row, length, block = span_info
        row_block = lax.dynamic_slice_in_dim(padded, start_row, SPAN_MOST, 0)
        weight_in = lax.dynamic_index_in_dim(input_rows, block, 0, keepdims=False)
        weight_out = lax.dynamic_index_in_dim(output_row_block, block, 0, keepdims=False)
        down_project = jnp.dot(row_block, jnp.transpose(weight_in), preferred_element_type=jnp.float32).astype(jnp.bfloat16)
        up_project = jnp.dot(down_project, weight_out, preferred_element_type=jnp.float32).astype(jnp.bfloat16)
        current = lax.dynamic_slice_in_dim(output_rows, start_row, SPAN_MOST, 0)
        merged = jnp.where((offsets < length)[:, None], up_project.astype(output_rows.dtype), current)
        return lax.dynamic_update_slice_in_dim(output_rows, merged, start_row, 0), None

    initial = jnp.zeros((TOKENS + SPAN_MOST, MODEL_WIDTH), tokens.dtype)
    final_rows, _ = lax.scan(apply_span, initial, (span_starts, lengths, storage))
    return final_rows[:TOKENS]
```

```python
import jax
import jax.numpy as jnp
from jax import lax
from jax.sharding import PartitionSpec as P

ADAPTER_RANK = 64


def route(slot_adapter_index, slot_token_length, adapter_block_table, tok_count, hot_rows):
    catalog = jnp.arange(adapter_block_table.shape[0], dtype=jnp.int32)
    position = jnp.sum(
        jnp.where(slot_adapter_index[:, None] == catalog[None, :], adapter_block_table[None, :], 0),
        axis=1,
    )
    span_ends = jnp.cumsum(slot_token_length)
    span_starts = span_ends - slot_token_length
    token_index = jnp.arange(hot_rows, tok_count, dtype=jnp.int32)
    inside = (token_index[:, None] >= span_starts[None, :]) & (
        token_index[:, None] < span_ends[None, :]
    )
    block = jnp.sum(jnp.where(inside, position[None, :], 0), axis=1)
    return position[0], block


def rank_among(owner):
    index = jnp.arange(owner.shape[0], dtype=jnp.int32)
    earlier = (owner[None, :] == owner[:, None]) & (index[None, :] < index[:, None])
    return jnp.sum(earlier.astype(jnp.int32), axis=1)


def hot_weights(hot_block, down_weight, up_weight, loaded_block):
    mine = hot_block // loaded_block == lax.axis_index("adapter")
    start = (hot_block % loaded_block) * ADAPTER_RANK
    down = lax.dynamic_slice_in_dim(down_weight, start, ADAPTER_RANK, 1)
    up = lax.dynamic_slice_in_dim(up_weight, start, ADAPTER_RANK, 0)
    down = lax.psum(jnp.where(mine, down, 0), "adapter")
    up = lax.psum(jnp.where(mine, up, 0), "adapter")
    return down, up


def apply_pair(rows, down, up):
    shrink = jnp.dot(rows, down, preferred_element_type=jnp.float32).astype(jnp.bfloat16)
    return jnp.dot(shrink, up, preferred_element_type=jnp.float32).astype(jnp.bfloat16)


def on_device(
    tokens, down_weight, up_weight, slot_adapter_index, slot_token_length, adapter_block_table
):
    devices = lax.axis_size("adapter")
    tok_count, width = tokens.shape
    hot_rows = 3 * tok_count // devices
    cap = hot_rows // 2
    loaded_block = down_weight.shape[1] // ADAPTER_RANK
    hot_block, block = route(
        slot_adapter_index, slot_token_length, adapter_block_table, tok_count, hot_rows
    )
    hot_down, hot_up = hot_weights(hot_block, down_weight, up_weight, loaded_block)
    cold = tokens[hot_rows:]
    owner = block // loaded_block
    slot_of_token = owner * cap + rank_among(owner)
    slot_index = jnp.arange(devices * cap, dtype=jnp.int32)
    hit = slot_index[:, None] == slot_of_token[None, :]
    pick = hit.astype(jnp.bfloat16)
    outgoing = jnp.dot(pick, cold, preferred_element_type=jnp.float32).astype(jnp.bfloat16)
    outgoing = outgoing.reshape(devices, cap, width)
    slot_tags = jnp.sum(jnp.where(hit, (block % loaded_block)[None, :], 0), axis=1)
    slot_tags = slot_tags.astype(jnp.bfloat16).reshape(devices, cap)
    incoming = lax.all_to_all(outgoing, "adapter", split_axis=0, concat_axis=0, tiled=True)
    tags = lax.all_to_all(slot_tags, "adapter", split_axis=0, concat_axis=0, tiled=True)
    rows = incoming.reshape(devices * cap, width)
    shrink = jnp.dot(rows, down_weight, preferred_element_type=jnp.float32)
    column_slot = jnp.arange(loaded_block * ADAPTER_RANK, dtype=jnp.int32) // ADAPTER_RANK
    keep = tags.reshape(-1).astype(jnp.int32)[:, None] == column_slot[None, :]
    shrink = jnp.where(keep, shrink, 0.0).astype(jnp.bfloat16)
    update = jnp.dot(shrink, up_weight, preferred_element_type=jnp.float32).astype(jnp.bfloat16)
    update = update.reshape(devices, cap, width)
    returned = lax.all_to_all(update, "adapter", split_axis=0, concat_axis=0, tiled=True)
    returned = returned.reshape(devices * cap, width)
    cold_update = jnp.dot(pick.T, returned, preferred_element_type=jnp.float32)
    hot_update = apply_pair(tokens[:hot_rows], hot_down, hot_up)
    return jnp.concatenate([hot_update, cold_update.astype(jnp.bfloat16)], axis=0)


def solution(mesh):
    in_specs = (
        P(("groups", "adapter"), None),
        P(None, "adapter"),
        P("adapter", None),
        P(("groups", "adapter")),
        P(("groups", "adapter")),
        P("groups"),
    )
    out_specs = P(("groups", "adapter"), None)
    return jax.shard_map(
        on_device, mesh=mesh, in_specs=in_specs, out_specs=out_specs, check_vma=False
    )
```

```python
import jax
import jax.numpy as jnp
from jax import lax
from jax.experimental import pallas as pl
from jax.experimental.pallas import tpu as pltpu
from jax.sharding import PartitionSpec as P

ADAPTER_RANK = 64


def route(slot_adapter_index, slot_token_length, adapter_block_table, tok_count, hot_rows):
    catalog = jnp.arange(adapter_block_table.shape[0], dtype=jnp.int32)
    position = jnp.sum(
        jnp.where(slot_adapter_index[:, None] == catalog[None, :], adapter_block_table[None, :], 0),
        axis=1,
    )
    span_ends = jnp.cumsum(slot_token_length)
    span_starts = span_ends - slot_token_length
    token_index = jnp.arange(hot_rows, tok_count, dtype=jnp.int32)
    inside = (token_index[:, None] >= span_starts[None, :]) & (
        token_index[:, None] < span_ends[None, :]
    )
    block = jnp.sum(jnp.where(inside, position[None, :], 0), axis=1)
    return position[0], block


def rank_among(owner):
    index = jnp.arange(owner.shape[0], dtype=jnp.int32)
    earlier = (owner[None, :] == owner[:, None]) & (index[None, :] < index[:, None])
    return jnp.sum(earlier.astype(jnp.int32), axis=1)


def hot_weights(hot_block, down_weight, up_weight, loaded_block):
    mine = hot_block // loaded_block == lax.axis_index("adapter")
    start = (hot_block % loaded_block) * ADAPTER_RANK
    down = lax.dynamic_slice_in_dim(down_weight, start, ADAPTER_RANK, 1)
    up = lax.dynamic_slice_in_dim(up_weight, start, ADAPTER_RANK, 0)
    down = lax.psum(jnp.where(mine, down, 0), "adapter")
    up = lax.psum(jnp.where(mine, up, 0), "adapter")
    return down, up


def apply_pair(rows, down, up):
    shrink = jnp.dot(rows, down, preferred_element_type=jnp.float32).astype(jnp.bfloat16)
    return jnp.dot(shrink, up, preferred_element_type=jnp.float32).astype(jnp.bfloat16)


def exchange_all(
    tokens, down_weight, up_weight, slot_adapter_index, slot_token_length, adapter_block_table
):
    devices = lax.axis_size("adapter")
    tok_count, width = tokens.shape
    hot_rows = 3 * tok_count // devices
    cap = hot_rows // 2
    loaded_block = down_weight.shape[1] // ADAPTER_RANK
    hot_block, block = route(
        slot_adapter_index, slot_token_length, adapter_block_table, tok_count, hot_rows
    )
    hot_down, hot_up = hot_weights(hot_block, down_weight, up_weight, loaded_block)
    cold = tokens[hot_rows:]
    owner = block // loaded_block
    slot_of_token = owner * cap + rank_among(owner)
    slot_index = jnp.arange(devices * cap, dtype=jnp.int32)
    hit = slot_index[:, None] == slot_of_token[None, :]
    pick = hit.astype(jnp.bfloat16)
    outgoing = jnp.dot(pick, cold, preferred_element_type=jnp.float32).astype(jnp.bfloat16)
    outgoing = outgoing.reshape(devices, cap, width)
    slot_tags = jnp.sum(jnp.where(hit, (block % loaded_block)[None, :], 0), axis=1)
    slot_tags = slot_tags.astype(jnp.bfloat16).reshape(devices, cap)
    incoming = lax.all_to_all(outgoing, "adapter", split_axis=0, concat_axis=0, tiled=True)
    tags = lax.all_to_all(slot_tags, "adapter", split_axis=0, concat_axis=0, tiled=True)
    rows = incoming.reshape(devices * cap, width)
    shrink = jnp.dot(rows, down_weight, preferred_element_type=jnp.float32)
    column_slot = jnp.arange(loaded_block * ADAPTER_RANK, dtype=jnp.int32) // ADAPTER_RANK
    keep = tags.reshape(-1).astype(jnp.int32)[:, None] == column_slot[None, :]
    shrink = jnp.where(keep, shrink, 0.0).astype(jnp.bfloat16)
    update = jnp.dot(shrink, up_weight, preferred_element_type=jnp.float32).astype(jnp.bfloat16)
    update = update.reshape(devices, cap, width)
    returned = lax.all_to_all(update, "adapter", split_axis=0, concat_axis=0, tiled=True)
    returned = returned.reshape(devices * cap, width)
    cold_update = jnp.dot(pick.T, returned, preferred_element_type=jnp.float32)
    hot_update = apply_pair(tokens[:hot_rows], hot_down, hot_up)
    return jnp.concatenate([hot_update, cold_update.astype(jnp.bfloat16)], axis=0)


PLANE = 4
LINE = 4
MESH = pl.DeviceIdType.MESH


def plane_kernel(
    cap, out_ref, tag_ref, down_ref, up_ref, ret_ref,
    rows, tags, down, up, result,
    local_sem, tok_send, tok_recv, tag_send, tag_recv,
    right_send, left_send, x_send, z_recv, x_recv, ret_send, ret_recv, own_sem,
):
    group = lax.axis_index("groups")
    me = lax.axis_index("adapter")
    z = me // PLANE
    q = me % PLANE
    other = 1 - group
    width = rows.shape[2]
    half_down = down.shape[1] // 2
    half_up = up.shape[1] // 2

    def peer(e):
        return (q + e) % PLANE

    own = [
        pltpu.make_async_copy(down_ref, down.at[z], local_sem.at[0]),
        pltpu.make_async_copy(up_ref, up.at[z], local_sem.at[1]),
        pltpu.make_async_copy(out_ref.at[q], rows.at[q], local_sem.at[2]),
        pltpu.make_async_copy(tag_ref.at[q], tags.at[q], local_sem.at[3]),
    ]
    for copy in own:
        copy.start()

    barrier = pltpu.get_barrier_semaphore()
    for e in range(1, PLANE):
        pl.semaphore_signal(
            barrier, inc=1, device_id=(group, z * PLANE + peer(e)), device_id_type=MESH
        )
    pl.semaphore_signal(barrier, inc=1, device_id=(other, me), device_id_type=MESH)

    @pl.when(z > 0)
    def _():
        pl.semaphore_signal(barrier, inc=1, device_id=(group, me - PLANE), device_id_type=MESH)

    @pl.when(z < LINE - 1)
    def _():
        pl.semaphore_signal(barrier, inc=1, device_id=(group, me + PLANE), device_id_type=MESH)

    pl.semaphore_wait(barrier, PLANE + 1 + (z % (LINE - 1) + LINE - 2) // (LINE - 1))

    for copy in own[:2]:
        copy.wait()

    def part(kind, origin, half):
        if kind == 0:
            return down.at[origin, pl.ds(pl.multiple_of(half * half_down, 128), half_down), :]
        return up.at[origin, pl.ds(pl.multiple_of(half * half_up, 16), half_up), :]

    def remote(kind, origin, half, send, recv, device):
        ref = part(kind, origin, half)
        return pltpu.make_async_remote_copy(
            src_ref=ref, dst_ref=ref,
            send_sem=send.at[origin, kind], recv_sem=recv.at[origin, kind],
            device_id=device, device_id_type=MESH,
        )

    def to_right(kind, origin):
        return remote(kind, origin, group, right_send, z_recv, (group, me + PLANE))

    def to_left(kind, origin):
        return remote(kind, origin, group, left_send, z_recv, (group, me - PLANE))

    def to_other(kind, origin):
        return remote(kind, origin, group, x_send, x_recv, (other, me))

    def from_other(kind, origin):
        return remote(kind, origin, other, x_send, x_recv, (other, me))

    for kind in range(2):
        @pl.when(z < LINE - 1)
        def _():
            to_right(kind, z).start()

        @pl.when(z > 0)
        def _():
            to_left(kind, z).start()

    def token_copy(e, slot):
        return pltpu.make_async_remote_copy(
            src_ref=out_ref.at[peer(e)], dst_ref=rows.at[slot],
            send_sem=tok_send.at[e], recv_sem=tok_recv.at[e],
            device_id=(group, z * PLANE + peer(e)), device_id_type=MESH,
        )

    def tag_copy(e, slot):
        return pltpu.make_async_remote_copy(
            src_ref=tag_ref.at[peer(e)], dst_ref=tags.at[slot],
            send_sem=tag_send.at[e], recv_sem=tag_recv.at[e],
            device_id=(group, z * PLANE + peer(e)), device_id_type=MESH,
        )

    for e in range(1, PLANE):
        tag_copy(e, q).start()
        token_copy(e, q).start()

    def pass_on(d):
        for kind in range(2):
            @pl.when(z >= d)
            def _():
                origin = z - d
                to_right_like = remote(kind, origin, group, right_send, z_recv, (other, me))
                to_right_like.wait_recv()
                to_other(kind, origin).start()

                @pl.when(z < LINE - 1)
                def _():
                    to_right(kind, origin).start()

            @pl.when(z + d < LINE)
            def _():
                origin = z + d
                to_left_like = remote(kind, origin, group, left_send, z_recv, (other, me))
                to_left_like.wait_recv()
                to_other(kind, origin).start()

                @pl.when(z > 0)
                def _():
                    to_left(kind, origin).start()

    def back(phase, first, count, e, slot):
        return pltpu.make_async_remote_copy(
            src_ref=result.at[peer(e), pl.ds(first, count), :],
            dst_ref=ret_ref.at[slot, pl.ds(first, count), :],
            send_sem=ret_send.at[phase, e], recv_sem=ret_recv.at[phase, e],
            device_id=(group, z * PLANE + peer(e)), device_id_type=MESH,
        )

    def keep_own(phase, first, count):
        return pltpu.make_async_copy(
            result.at[q, pl.ds(first, count), :],
            ret_ref.at[q, pl.ds(first, count), :],
            own_sem.at[phase],
        )

    def compute(phase, first, count, origins):
        step = 1024

        def shrink_step(t, sums):
            k = pl.ds(pl.multiple_of(t * step, step), step)
            x = rows[:, first : first + count, k].reshape(PLANE * count, step)
            return tuple(
                s + jnp.dot(x, down[o, k, :], preferred_element_type=jnp.float32)
                for s, o in zip(sums, origins)
            )

        lanes = down.shape[2]
        zero = jnp.zeros((PLANE * count, lanes), jnp.float32)
        sums = lax.fori_loop(0, width // step, shrink_step, tuple(zero for _ in origins))
        tag = tags[:, first : first + count, :].reshape(PLANE * count, lanes).astype(jnp.float32)
        slot = lax.broadcasted_iota(jnp.int32, (PLANE * count, lanes), 1) // ADAPTER_RANK
        tag = tag.astype(jnp.int32) - slot
        loaded = lanes // ADAPTER_RANK
        masked = [
            jnp.where(tag == o * loaded, s, 0.0).astype(jnp.bfloat16)
            for s, o in zip(sums, origins)
        ]
        tile = 512

        def up_step(t, carry):
            c = pl.ds(pl.multiple_of(t * tile, tile), tile)
            total = jnp.zeros((PLANE * count, tile), jnp.float32)
            for m, o in zip(masked, origins):
                total += jnp.dot(m, up[o, :, c], preferred_element_type=jnp.float32)
            result[:, first : first + count, c] = total.astype(jnp.bfloat16).reshape(
                PLANE, count, tile
            )
            return carry

        lax.fori_loop(0, width // tile, up_step, 0)
        for e in range(1, PLANE):
            back(phase, first, count, e, q).start()
        keep_own(phase, first, count).start()

    def arrive(origin):
        for kind in range(2):
            from_other(kind, origin).wait_recv()

    near = z + 1 - 2 * (z % 2)
    third = 2 - z // 2
    far = 3 * (1 - z // 2)
    phases = ((0, 2 * cap), (2 * cap, cap + 8), (3 * cap + 8, 2 * cap))

    pass_on(1)
    pass_on(2)
    for copy in own[2:]:
        copy.wait()
    for e in range(1, PLANE):
        tag_copy(e, (q + PLANE - e) % PLANE).wait_recv()
        token_copy(e, (q + PLANE - e) % PLANE).wait_recv()
    arrive(near)
    compute(0, *phases[0], (z, near))
    pass_on(3)
    arrive(third)
    compute(1, *phases[1], (third,))
    arrive(far)
    compute(2, *phases[2], (z, near, third, far))

    for e in range(1, PLANE):
        tag_copy(e, q).wait_send()
        token_copy(e, q).wait_send()
    for kind in range(2):
        for d in range(LINE):
            @pl.when((z >= d) & (z < LINE - 1))
            def _():
                to_right(kind, z - d).wait_send()

            @pl.when((z + d < LINE) & (z > 0))
            def _():
                to_left(kind, z + d).wait_send()

        for origin in (near, third, far):
            to_other(kind, origin).wait_send()
    for phase, (first, count) in enumerate(phases):
        keep_own(phase, first, count).wait()
        for e in range(1, PLANE):
            back(phase, first, count, e, q).wait_send()
            back(phase, first, count, e, (q + PLANE - e) % PLANE).wait_recv()


def exchange_planes(
    tokens, down_weight, up_weight, slot_adapter_index, slot_token_length, adapter_block_table
):
    devices = lax.axis_size("adapter")
    tok_count, width = tokens.shape
    cap = 3 * tok_count // devices // 2
    lanes = down_weight.shape[1]
    loaded_block = lanes // ADAPTER_RANK
    me = lax.axis_index("adapter")
    z = me // PLANE
    _, block = route(slot_adapter_index, slot_token_length, adapter_block_table, tok_count, 0)
    owner = block // loaded_block
    rank = rank_among(owner)
    origin = owner // PLANE
    near = z + 1 - 2 * (z % 2)
    third = 2 - z // 2
    base = jnp.where(
        origin == z,
        0,
        jnp.where(origin == near, cap, jnp.where(origin == third, 2 * cap, 3 * cap + 8)),
    )
    base = jnp.where(rank < cap, base, 3 * cap + 8)
    slots = 5 * cap + 8
    slot_of_token = (owner % PLANE) * slots + base + rank
    slot_index = jnp.arange(PLANE * slots, dtype=jnp.int32)
    hit = slot_index[:, None] == slot_of_token[None, :]
    pick = hit.astype(jnp.bfloat16)
    outgoing = jnp.dot(pick, tokens, preferred_element_type=jnp.float32).astype(jnp.bfloat16)
    outgoing = outgoing.reshape(PLANE, slots, width)
    tag = jnp.sum(jnp.where(hit, (origin * loaded_block + block % loaded_block)[None, :], 0), axis=1)
    tag = jnp.broadcast_to(tag.astype(jnp.bfloat16)[:, None], (PLANE * slots, lanes))
    tag = tag.reshape(PLANE, slots, lanes)
    dma = pltpu.SemaphoreType.DMA
    returned = pl.pallas_call(
        lambda *refs: plane_kernel(cap, *refs),
        out_shape=jax.ShapeDtypeStruct((PLANE, slots, width), jnp.bfloat16),
        in_specs=[pl.BlockSpec(memory_space=pl.ANY)] * 4,
        out_specs=pl.BlockSpec(memory_space=pl.ANY),
        scratch_shapes=[
            pltpu.VMEM((PLANE, slots, width), jnp.bfloat16),
            pltpu.VMEM((PLANE, slots, lanes), jnp.bfloat16),
            pltpu.VMEM((LINE, width, lanes), jnp.bfloat16),
            pltpu.VMEM((LINE, lanes, width), jnp.bfloat16),
            pltpu.VMEM((PLANE, slots, width), jnp.bfloat16),
            dma((4,)),
            dma((PLANE,)),
            dma((PLANE,)),
            dma((PLANE,)),
            dma((PLANE,)),
            dma((LINE, 2)),
            dma((LINE, 2)),
            dma((LINE, 2)),
            dma((LINE, 2)),
            dma((LINE, 2)),
            dma((3, PLANE)),
            dma((3, PLANE)),
            dma((3,)),
        ],
        compiler_params=pltpu.CompilerParams(
            collective_id=0, has_side_effects=True, vmem_limit_bytes=56 * 2**20
        ),
        cost_estimate=pl.CostEstimate(
            flops=8 * PLANE * slots * width * lanes,
            bytes_accessed=8 * PLANE * slots * width,
            transcendentals=0,
        ),
    )(outgoing, tag, down_weight, up_weight)
    returned = returned.reshape(PLANE * slots, width)
    update = jnp.dot(pick.T, returned, preferred_element_type=jnp.float32)
    return update.astype(jnp.bfloat16)


def solution(mesh):
    sizes = dict(mesh.shape)
    planes = sizes["groups"] == 2 and sizes["adapter"] == PLANE * LINE
    on_device = exchange_planes if planes else exchange_all
    in_specs = (
        P(("groups", "adapter"), None),
        P(None, "adapter"),
        P("adapter", None),
        P(("groups", "adapter")),
        P(("groups", "adapter")),
        P("groups"),
    )
    out_specs = P(("groups", "adapter"), None)
    return jax.shard_map(
        on_device, mesh=mesh, in_specs=in_specs, out_specs=out_specs, check_vma=False
    )
```

```python
import jax
import jax.numpy as jnp
from jax import lax
from jax.experimental import pallas as pl
from jax.experimental.pallas import tpu as pltpu
from jax.sharding import PartitionSpec as P

ADAPTER_RANK = 64


def route(slot_adapter_index, slot_token_length, adapter_block_table, tok_count, hot_rows):
    catalog = jnp.arange(adapter_block_table.shape[0], dtype=jnp.int32)
    position = jnp.sum(
        jnp.where(slot_adapter_index[:, None] == catalog[None, :], adapter_block_table[None, :], 0),
        axis=1,
    )
    span_ends = jnp.cumsum(slot_token_length)
    span_starts = span_ends - slot_token_length
    token_index = jnp.arange(hot_rows, tok_count, dtype=jnp.int32)
    inside = (token_index[:, None] >= span_starts[None, :]) & (
        token_index[:, None] < span_ends[None, :]
    )
    block = jnp.sum(jnp.where(inside, position[None, :], 0), axis=1)
    return position[0], block


def rank_among(owner):
    index = jnp.arange(owner.shape[0], dtype=jnp.int32)
    earlier = (owner[None, :] == owner[:, None]) & (index[None, :] < index[:, None])
    return jnp.sum(earlier.astype(jnp.int32), axis=1)


def hot_weights(hot_block, down_weight, up_weight, loaded_block):
    mine = hot_block // loaded_block == lax.axis_index("adapter")
    start = (hot_block % loaded_block) * ADAPTER_RANK
    down = lax.dynamic_slice_in_dim(down_weight, start, ADAPTER_RANK, 1)
    up = lax.dynamic_slice_in_dim(up_weight, start, ADAPTER_RANK, 0)
    down = lax.psum(jnp.where(mine, down, 0), "adapter")
    up = lax.psum(jnp.where(mine, up, 0), "adapter")
    return down, up


def apply_pair(rows, down, up):
    shrink = jnp.dot(rows, down, preferred_element_type=jnp.float32).astype(jnp.bfloat16)
    return jnp.dot(shrink, up, preferred_element_type=jnp.float32).astype(jnp.bfloat16)


def exchange_all(
    tokens, down_weight, up_weight, slot_adapter_index, slot_token_length, adapter_block_table
):
    devices = lax.axis_size("adapter")
    tok_count, width = tokens.shape
    hot_rows = 3 * tok_count // devices
    cap = hot_rows // 2
    loaded_block = down_weight.shape[1] // ADAPTER_RANK
    hot_block, block = route(
        slot_adapter_index, slot_token_length, adapter_block_table, tok_count, hot_rows
    )
    hot_down, hot_up = hot_weights(hot_block, down_weight, up_weight, loaded_block)
    cold = tokens[hot_rows:]
    owner = block // loaded_block
    slot_of_token = owner * cap + rank_among(owner)
    slot_index = jnp.arange(devices * cap, dtype=jnp.int32)
    hit = slot_index[:, None] == slot_of_token[None, :]
    pick = hit.astype(jnp.bfloat16)
    outgoing = jnp.dot(pick, cold, preferred_element_type=jnp.float32).astype(jnp.bfloat16)
    outgoing = outgoing.reshape(devices, cap, width)
    slot_tags = jnp.sum(jnp.where(hit, (block % loaded_block)[None, :], 0), axis=1)
    slot_tags = slot_tags.astype(jnp.bfloat16).reshape(devices, cap)
    incoming = lax.all_to_all(outgoing, "adapter", split_axis=0, concat_axis=0, tiled=True)
    tags = lax.all_to_all(slot_tags, "adapter", split_axis=0, concat_axis=0, tiled=True)
    rows = incoming.reshape(devices * cap, width)
    shrink = jnp.dot(rows, down_weight, preferred_element_type=jnp.float32)
    column_slot = jnp.arange(loaded_block * ADAPTER_RANK, dtype=jnp.int32) // ADAPTER_RANK
    keep = tags.reshape(-1).astype(jnp.int32)[:, None] == column_slot[None, :]
    shrink = jnp.where(keep, shrink, 0.0).astype(jnp.bfloat16)
    update = jnp.dot(shrink, up_weight, preferred_element_type=jnp.float32).astype(jnp.bfloat16)
    update = update.reshape(devices, cap, width)
    returned = lax.all_to_all(update, "adapter", split_axis=0, concat_axis=0, tiled=True)
    returned = returned.reshape(devices * cap, width)
    cold_update = jnp.dot(pick.T, returned, preferred_element_type=jnp.float32)
    hot_update = apply_pair(tokens[:hot_rows], hot_down, hot_up)
    return jnp.concatenate([hot_update, cold_update.astype(jnp.bfloat16)], axis=0)


PLANE = 4
LINE = 4
DOWN_PARTS = 2
MESH = pl.DeviceIdType.MESH


def plane_kernel(
    tiles, out_ref, tag_ref, down_ref, up_ref, ret_ref,
    rows, tags, down, up, result, shrink,
    local_sem, tok_send, tok_recv, tag_send, tag_recv,
    right_send, left_send, x_send, z_recv, x_recv, ret_send, ret_recv, own_sem,
):
    group = lax.axis_index("groups")
    me = lax.axis_index("adapter")
    z = me // PLANE
    q = me % PLANE
    other = 1 - group
    width = rows.shape[2]
    kinds = DOWN_PARTS + len(tiles)
    half_down = down.shape[1] // 2
    half_up = up.shape[1] // 2

    def peer(e):
        return (q + e) % PLANE

    own = [
        pltpu.make_async_copy(down_ref, down.at[z], local_sem.at[0]),
        pltpu.make_async_copy(up_ref, up.at[z], local_sem.at[1]),
        pltpu.make_async_copy(out_ref.at[q], rows.at[q], local_sem.at[2]),
        pltpu.make_async_copy(tag_ref.at[q], tags.at[q], local_sem.at[3]),
    ]
    for copy in own:
        copy.start()

    barrier = pltpu.get_barrier_semaphore()
    for e in range(1, PLANE):
        pl.semaphore_signal(
            barrier, inc=1, device_id=(group, z * PLANE + peer(e)), device_id_type=MESH
        )
    pl.semaphore_signal(barrier, inc=1, device_id=(other, me), device_id_type=MESH)

    @pl.when(z > 0)
    def _():
        pl.semaphore_signal(barrier, inc=1, device_id=(group, me - PLANE), device_id_type=MESH)

    @pl.when(z < LINE - 1)
    def _():
        pl.semaphore_signal(barrier, inc=1, device_id=(group, me + PLANE), device_id_type=MESH)

    pl.semaphore_wait(barrier, PLANE + 1 + (z % (LINE - 1) + LINE - 2) // (LINE - 1))

    for copy in own[:2]:
        copy.wait()

    def part(kind, origin, half):
        if kind < DOWN_PARTS:
            count = half_down // DOWN_PARTS
            start = half * half_down + kind * count
            return down.at[origin, pl.ds(pl.multiple_of(start, 128), count), :]
        first, count = tiles[kind - DOWN_PARTS]
        lines = pl.ds(pl.multiple_of(half * half_up, 16), half_up)
        return up.at[origin, lines, pl.ds(first, count)]

    def remote(kind, origin, half, send, recv, device):
        ref = part(kind, origin, half)
        return pltpu.make_async_remote_copy(
            src_ref=ref, dst_ref=ref,
            send_sem=send.at[origin, kind], recv_sem=recv.at[origin, kind],
            device_id=device, device_id_type=MESH,
        )

    def to_right(kind, origin):
        return remote(kind, origin, group, right_send, z_recv, (group, me + PLANE))

    def to_left(kind, origin):
        return remote(kind, origin, group, left_send, z_recv, (group, me - PLANE))

    def to_other(kind, origin):
        return remote(kind, origin, group, x_send, x_recv, (other, me))

    def from_other(kind, origin):
        return remote(kind, origin, other, x_send, x_recv, (other, me))

    def send_own(kind):
        @pl.when(z < LINE - 1)
        def _():
            to_right(kind, z).start()

        @pl.when(z > 0)
        def _():
            to_left(kind, z).start()

    send_own(0)
    send_own(1)

    def token_copy(e, slot):
        return pltpu.make_async_remote_copy(
            src_ref=out_ref.at[peer(e)], dst_ref=rows.at[slot],
            send_sem=tok_send.at[e], recv_sem=tok_recv.at[e],
            device_id=(group, z * PLANE + peer(e)), device_id_type=MESH,
        )

    def tag_copy(e, slot):
        return pltpu.make_async_remote_copy(
            src_ref=tag_ref.at[peer(e)], dst_ref=tags.at[slot],
            send_sem=tag_send.at[e], recv_sem=tag_recv.at[e],
            device_id=(group, z * PLANE + peer(e)), device_id_type=MESH,
        )

    for e in range(1, PLANE):
        tag_copy(e, q).start()
        token_copy(e, q).start()

    def pass_on(kind):
        if kind + 2 < kinds:
            send_own(kind + 2)
        for d in range(1, LINE):
            @pl.when(z >= d)
            def _():
                origin = z - d
                remote(kind, origin, group, right_send, z_recv, (other, me)).wait_recv()

                @pl.when(z < LINE - 1)
                def _():
                    to_right(kind, origin).start()

                to_other(kind, origin).start()

            @pl.when(z + d < LINE)
            def _():
                origin = z + d
                remote(kind, origin, group, left_send, z_recv, (other, me)).wait_recv()

                @pl.when(z > 0)
                def _():
                    to_left(kind, origin).start()

                to_other(kind, origin).start()

    def back(t, e, slot):
        columns = pl.ds(*tiles[t])
        return pltpu.make_async_remote_copy(
            src_ref=result.at[peer(e), :, columns],
            dst_ref=ret_ref.at[slot, :, columns],
            send_sem=ret_send.at[t, e], recv_sem=ret_recv.at[t, e],
            device_id=(group, z * PLANE + peer(e)), device_id_type=MESH,
        )

    def keep_own(t):
        columns = pl.ds(*tiles[t])
        return pltpu.make_async_copy(
            result.at[q, :, columns], ret_ref.at[q, :, columns], own_sem.at[t]
        )

    slots = rows.shape[1]
    lanes = down.shape[2]
    total_rows = PLANE * slots
    origins = (z, z + 1 - 2 * (z % 2), 2 - z // 2, 3 * (1 - z // 2))

    def arrive(kind):
        for origin in origins[1:]:
            from_other(kind, origin).wait_recv()

    def shrink_all():
        step = 1024
        tag = tags[...].reshape(total_rows, lanes).astype(jnp.int32)
        tag = tag - lax.broadcasted_iota(jnp.int32, (total_rows, lanes), 1) // ADAPTER_RANK

        def shrink_origin(o, carry):
            def shrink_step(t, total):
                k = pl.ds(pl.multiple_of(t * step, step), step)
                x = rows[:, :, k].reshape(total_rows, step)
                return total + jnp.dot(x, down[o, k, :], preferred_element_type=jnp.float32)

            zero = jnp.zeros((total_rows, lanes), jnp.float32)
            total = lax.fori_loop(0, width // step, shrink_step, zero)
            kept = jnp.where(tag == o * (lanes // ADAPTER_RANK), total, 0.0)
            shrink[o] = kept.astype(jnp.bfloat16)
            return carry

        lax.fori_loop(0, LINE, shrink_origin, 0)

    def expand(t):
        first, count = tiles[t]
        tile = 512

        def up_step(i, carry):
            c = pl.ds(pl.multiple_of(first + i * tile, tile), tile)
            total = jnp.zeros((total_rows, tile), jnp.float32)
            for o in range(LINE):
                total += jnp.dot(shrink[o], up[o, :, c], preferred_element_type=jnp.float32)
            result[:, :, c] = total.astype(jnp.bfloat16).reshape(PLANE, slots, tile)
            return carry

        lax.fori_loop(0, count // tile, up_step, 0)
        for e in range(1, PLANE):
            back(t, e, q).start()
        keep_own(t).start()

    for kind in range(DOWN_PARTS + 1):
        pass_on(kind)
    for copy in own[2:]:
        copy.wait()
    for e in range(1, PLANE):
        tag_copy(e, (q + PLANE - e) % PLANE).wait_recv()
        token_copy(e, (q + PLANE - e) % PLANE).wait_recv()
    for kind in range(DOWN_PARTS):
        arrive(kind)
    shrink_all()
    for t in range(len(tiles)):
        if t + 1 < len(tiles):
            pass_on(DOWN_PARTS + t + 1)
        arrive(DOWN_PARTS + t)
        expand(t)

    for e in range(1, PLANE):
        tag_copy(e, q).wait_send()
        token_copy(e, q).wait_send()
    for kind in range(kinds):
        for d in range(LINE):
            @pl.when((z >= d) & (z < LINE - 1))
            def _():
                to_right(kind, z - d).wait_send()

            @pl.when((z + d < LINE) & (z > 0))
            def _():
                to_left(kind, z + d).wait_send()

        for origin in origins[1:]:
            to_other(kind, origin).wait_send()
    for t in range(len(tiles)):
        keep_own(t).wait()
        for e in range(1, PLANE):
            back(t, e, q).wait_send()
            back(t, e, (q + PLANE - e) % PLANE).wait_recv()


def exchange_planes(
    tokens, down_weight, up_weight, slot_adapter_index, slot_token_length, adapter_block_table
):
    devices = lax.axis_size("adapter")
    tok_count, width = tokens.shape
    cap = 3 * tok_count // devices // 2
    lanes = down_weight.shape[1]
    loaded_block = lanes // ADAPTER_RANK
    me = lax.axis_index("adapter")
    z = me // PLANE
    _, block = route(slot_adapter_index, slot_token_length, adapter_block_table, tok_count, 0)
    owner = block // loaded_block
    rank = rank_among(owner)
    origin = owner // PLANE
    near = z + 1 - 2 * (z % 2)
    third = 2 - z // 2
    base = jnp.where(
        origin == z,
        0,
        jnp.where(origin == near, cap, jnp.where(origin == third, 2 * cap, 3 * cap + 8)),
    )
    base = jnp.where(rank < cap, base, 3 * cap + 8)
    slots = 5 * cap + 8
    slot_of_token = (owner % PLANE) * slots + base + rank
    slot_index = jnp.arange(PLANE * slots, dtype=jnp.int32)
    hit = slot_index[:, None] == slot_of_token[None, :]
    pick = hit.astype(jnp.bfloat16)
    outgoing = jnp.dot(pick, tokens, preferred_element_type=jnp.float32).astype(jnp.bfloat16)
    outgoing = outgoing.reshape(PLANE, slots, width)
    tag = jnp.sum(jnp.where(hit, (origin * loaded_block + block % loaded_block)[None, :], 0), axis=1)
    tag = jnp.broadcast_to(tag.astype(jnp.bfloat16)[:, None], (PLANE * slots, lanes))
    tag = tag.reshape(PLANE, slots, lanes)
    dma = pltpu.SemaphoreType.DMA
    eighth = width // 8
    tiles = [(0, eighth), (eighth, eighth)] + [(i * eighth, 2 * eighth) for i in (2, 4, 6)]
    kinds = DOWN_PARTS + len(tiles)
    returned = pl.pallas_call(
        lambda *refs: plane_kernel(tiles, *refs),
        out_shape=jax.ShapeDtypeStruct((PLANE, slots, width), jnp.bfloat16),
        in_specs=[pl.BlockSpec(memory_space=pl.ANY)] * 4,
        out_specs=pl.BlockSpec(memory_space=pl.ANY),
        scratch_shapes=[
            pltpu.VMEM((PLANE, slots, width), jnp.bfloat16),
            pltpu.VMEM((PLANE, slots, lanes), jnp.bfloat16),
            pltpu.VMEM((LINE, width, lanes), jnp.bfloat16),
            pltpu.VMEM((LINE, lanes, width), jnp.bfloat16),
            pltpu.VMEM((PLANE, slots, width), jnp.bfloat16),
            pltpu.VMEM((LINE, PLANE * slots, lanes), jnp.bfloat16),
            dma((4,)),
            dma((PLANE,)),
            dma((PLANE,)),
            dma((PLANE,)),
            dma((PLANE,)),
            dma((LINE, kinds)),
            dma((LINE, kinds)),
            dma((LINE, kinds)),
            dma((LINE, kinds)),
            dma((LINE, kinds)),
            dma((len(tiles), PLANE)),
            dma((len(tiles), PLANE)),
            dma((len(tiles),)),
        ],
        compiler_params=pltpu.CompilerParams(
            collective_id=0, has_side_effects=True, vmem_limit_bytes=56 * 2**20
        ),
        cost_estimate=pl.CostEstimate(
            flops=8 * PLANE * slots * width * lanes,
            bytes_accessed=8 * PLANE * slots * width,
            transcendentals=0,
        ),
    )(outgoing, tag, down_weight, up_weight)
    returned = returned.reshape(PLANE * slots, width)
    update = jnp.dot(pick.T, returned, preferred_element_type=jnp.float32)
    return update.astype(jnp.bfloat16)


def solution(mesh):
    sizes = dict(mesh.shape)
    planes = sizes["groups"] == 2 and sizes["adapter"] == PLANE * LINE
    on_device = exchange_planes if planes else exchange_all
    in_specs = (
        P(("groups", "adapter"), None),
        P(None, "adapter"),
        P("adapter", None),
        P(("groups", "adapter")),
        P(("groups", "adapter")),
        P("groups"),
    )
    out_specs = P(("groups", "adapter"), None)
    return jax.shard_map(
        on_device, mesh=mesh, in_specs=in_specs, out_specs=out_specs, check_vma=False
    )
```

```python
import jax
import jax.numpy as jnp
from jax import lax
from jax.experimental import pallas as pl
from jax.experimental.pallas import tpu as pltpu
from jax.sharding import PartitionSpec as P

ADAPTER_RANK = 64


def route(slot_adapter_index, slot_token_length, adapter_block_table, tok_count, hot_rows):
    catalog = jnp.arange(adapter_block_table.shape[0], dtype=jnp.int32)
    position = jnp.sum(
        jnp.where(slot_adapter_index[:, None] == catalog[None, :], adapter_block_table[None, :], 0),
        axis=1,
    )
    span_ends = jnp.cumsum(slot_token_length)
    span_starts = span_ends - slot_token_length
    token_index = jnp.arange(hot_rows, tok_count, dtype=jnp.int32)
    inside = (token_index[:, None] >= span_starts[None, :]) & (
        token_index[:, None] < span_ends[None, :]
    )
    block = jnp.sum(jnp.where(inside, position[None, :], 0), axis=1)
    return position[0], block


def rank_among(owner):
    index = jnp.arange(owner.shape[0], dtype=jnp.int32)
    earlier = (owner[None, :] == owner[:, None]) & (index[None, :] < index[:, None])
    return jnp.sum(earlier.astype(jnp.int32), axis=1)


def hot_weights(hot_block, down_weight, up_weight, loaded_block):
    mine = hot_block // loaded_block == lax.axis_index("adapter")
    start = (hot_block % loaded_block) * ADAPTER_RANK
    down = lax.dynamic_slice_in_dim(down_weight, start, ADAPTER_RANK, 1)
    up = lax.dynamic_slice_in_dim(up_weight, start, ADAPTER_RANK, 0)
    down = lax.psum(jnp.where(mine, down, 0), "adapter")
    up = lax.psum(jnp.where(mine, up, 0), "adapter")
    return down, up


def apply_pair(rows, down, up):
    shrink = jnp.dot(rows, down, preferred_element_type=jnp.float32).astype(jnp.bfloat16)
    return jnp.dot(shrink, up, preferred_element_type=jnp.float32).astype(jnp.bfloat16)


def exchange_all(
    tokens, down_weight, up_weight, slot_adapter_index, slot_token_length, adapter_block_table
):
    devices = lax.axis_size("adapter")
    tok_count, width = tokens.shape
    hot_rows = 3 * tok_count // devices
    cap = hot_rows // 2
    loaded_block = down_weight.shape[1] // ADAPTER_RANK
    hot_block, block = route(
        slot_adapter_index, slot_token_length, adapter_block_table, tok_count, hot_rows
    )
    hot_down, hot_up = hot_weights(hot_block, down_weight, up_weight, loaded_block)
    cold = tokens[hot_rows:]
    owner = block // loaded_block
    slot_of_token = owner * cap + rank_among(owner)
    slot_index = jnp.arange(devices * cap, dtype=jnp.int32)
    hit = slot_index[:, None] == slot_of_token[None, :]
    pick = hit.astype(jnp.bfloat16)
    outgoing = jnp.dot(pick, cold, preferred_element_type=jnp.float32).astype(jnp.bfloat16)
    outgoing = outgoing.reshape(devices, cap, width)
    slot_tags = jnp.sum(jnp.where(hit, (block % loaded_block)[None, :], 0), axis=1)
    slot_tags = slot_tags.astype(jnp.bfloat16).reshape(devices, cap)
    incoming = lax.all_to_all(outgoing, "adapter", split_axis=0, concat_axis=0, tiled=True)
    tags = lax.all_to_all(slot_tags, "adapter", split_axis=0, concat_axis=0, tiled=True)
    rows = incoming.reshape(devices * cap, width)
    shrink = jnp.dot(rows, down_weight, preferred_element_type=jnp.float32)
    column_slot = jnp.arange(loaded_block * ADAPTER_RANK, dtype=jnp.int32) // ADAPTER_RANK
    keep = tags.reshape(-1).astype(jnp.int32)[:, None] == column_slot[None, :]
    shrink = jnp.where(keep, shrink, 0.0).astype(jnp.bfloat16)
    update = jnp.dot(shrink, up_weight, preferred_element_type=jnp.float32).astype(jnp.bfloat16)
    update = update.reshape(devices, cap, width)
    returned = lax.all_to_all(update, "adapter", split_axis=0, concat_axis=0, tiled=True)
    returned = returned.reshape(devices * cap, width)
    cold_update = jnp.dot(pick.T, returned, preferred_element_type=jnp.float32)
    hot_update = apply_pair(tokens[:hot_rows], hot_down, hot_up)
    return jnp.concatenate([hot_update, cold_update.astype(jnp.bfloat16)], axis=0)


PLANE = 4
LINE = 4
DOWN_PARTS = 4
MESH = pl.DeviceIdType.MESH


def plane_kernel(
    tiles, tokens_ref, pick_ref, tag_ref, down_ref, up_ref, ret_ref,
    stage, rows, tags, down, up, result, sums, shrink,
    local_sem, tok_own, tok_send, tok_recv, tag_send, tag_recv,
    right_send, left_send, x_send, z_recv, x_recv, ret_send, ret_recv, own_sem,
):
    group = lax.axis_index("groups")
    me = lax.axis_index("adapter")
    z = me // PLANE
    q = me % PLANE
    other = 1 - group
    width = rows.shape[2]
    kinds = DOWN_PARTS + len(tiles)
    half_down = down.shape[1] // 2
    half_up = up.shape[1] // 2

    def peer(e):
        return (q + e) % PLANE

    own = [
        pltpu.make_async_copy(down_ref, down.at[z], local_sem.at[0]),
        pltpu.make_async_copy(up_ref, up.at[z], local_sem.at[1]),
        pltpu.make_async_copy(tag_ref.at[q], tags.at[q], local_sem.at[2]),
    ]
    for copy in own:
        copy.start()

    barrier = pltpu.get_barrier_semaphore()
    for e in range(1, PLANE):
        pl.semaphore_signal(
            barrier, inc=1, device_id=(group, z * PLANE + peer(e)), device_id_type=MESH
        )
    pl.semaphore_signal(barrier, inc=1, device_id=(other, me), device_id_type=MESH)

    @pl.when(z > 0)
    def _():
        pl.semaphore_signal(barrier, inc=1, device_id=(group, me - PLANE), device_id_type=MESH)

    @pl.when(z < LINE - 1)
    def _():
        pl.semaphore_signal(barrier, inc=1, device_id=(group, me + PLANE), device_id_type=MESH)

    pl.semaphore_wait(barrier, PLANE + 1 + (z % (LINE - 1) + LINE - 2) // (LINE - 1))

    for copy in own[:2]:
        copy.wait()

    def part(kind, origin, half):
        if kind < DOWN_PARTS:
            count = half_down // DOWN_PARTS
            start = half * half_down + kind * count
            return down.at[origin, pl.ds(pl.multiple_of(start, 128), count), :]
        first, count = tiles[kind - DOWN_PARTS]
        lines = pl.ds(pl.multiple_of(half * half_up, 16), half_up)
        return up.at[origin, lines, pl.ds(first, count)]

    def remote(kind, origin, half, send, recv, device):
        ref = part(kind, origin, half)
        return pltpu.make_async_remote_copy(
            src_ref=ref, dst_ref=ref,
            send_sem=send.at[origin, kind], recv_sem=recv.at[origin, kind],
            device_id=device, device_id_type=MESH,
        )

    def to_right(kind, origin):
        return remote(kind, origin, group, right_send, z_recv, (group, me + PLANE))

    def to_left(kind, origin):
        return remote(kind, origin, group, left_send, z_recv, (group, me - PLANE))

    def to_other(kind, origin):
        return remote(kind, origin, group, x_send, x_recv, (other, me))

    def from_other(kind, origin):
        return remote(kind, origin, other, x_send, x_recv, (other, me))

    def send_own(kind):
        @pl.when(z < LINE - 1)
        def _():
            to_right(kind, z).start()

        @pl.when(z > 0)
        def _():
            to_left(kind, z).start()

    send_own(0)
    send_own(1)

    step = half_down // DOWN_PARTS
    slots = rows.shape[1]
    lanes = down.shape[2]
    total_rows = PLANE * slots

    def token_copy(t, e, slot):
        columns = pl.ds(t * step, step)
        return pltpu.make_async_remote_copy(
            src_ref=stage.at[peer(e), :, columns], dst_ref=rows.at[slot, :, columns],
            send_sem=tok_send.at[t, e], recv_sem=tok_recv.at[t, e],
            device_id=(group, z * PLANE + peer(e)), device_id_type=MESH,
        )

    def token_own(t):
        columns = pl.ds(t * step, step)
        return pltpu.make_async_copy(
            stage.at[q, :, columns], rows.at[q, :, columns], tok_own.at[t]
        )

    def tag_copy(e, slot):
        return pltpu.make_async_remote_copy(
            src_ref=tag_ref.at[peer(e)], dst_ref=tags.at[slot],
            send_sem=tag_send.at[e], recv_sem=tag_recv.at[e],
            device_id=(group, z * PLANE + peer(e)), device_id_type=MESH,
        )

    for e in range(1, PLANE):
        tag_copy(e, q).start()

    def send_tokens(t):
        picked = jnp.dot(
            pick_ref[...], tokens_ref[:, t * step : (t + 1) * step],
            preferred_element_type=jnp.float32,
        )
        stage[:, :, t * step : (t + 1) * step] = picked.astype(jnp.bfloat16).reshape(
            PLANE, slots, step
        )
        for e in range(1, PLANE):
            token_copy(t, e, q).start()
        token_own(t).start()

    for part_at in range(DOWN_PARTS):
        send_tokens(part_at)
        send_tokens(part_at + DOWN_PARTS)

    def pass_on(kind):
        if kind + 2 < kinds:
            send_own(kind + 2)
        for d in range(1, LINE):
            @pl.when(z >= d)
            def _():
                origin = z - d
                remote(kind, origin, group, right_send, z_recv, (other, me)).wait_recv()

                @pl.when(z < LINE - 1)
                def _():
                    to_right(kind, origin).start()

                to_other(kind, origin).start()

            @pl.when(z + d < LINE)
            def _():
                origin = z + d
                remote(kind, origin, group, left_send, z_recv, (other, me)).wait_recv()

                @pl.when(z > 0)
                def _():
                    to_left(kind, origin).start()

                to_other(kind, origin).start()

    def back(t, e, slot):
        columns = pl.ds(*tiles[t])
        return pltpu.make_async_remote_copy(
            src_ref=result.at[peer(e), :, columns],
            dst_ref=ret_ref.at[slot, :, columns],
            send_sem=ret_send.at[t, e], recv_sem=ret_recv.at[t, e],
            device_id=(group, z * PLANE + peer(e)), device_id_type=MESH,
        )

    def keep_own(t):
        columns = pl.ds(*tiles[t])
        return pltpu.make_async_copy(
            result.at[q, :, columns], ret_ref.at[q, :, columns], own_sem.at[t]
        )

    origins = (z, z + 1 - 2 * (z % 2), 2 - z // 2, 3 * (1 - z // 2))

    def arrive(kind):
        for origin in origins[1:]:
            from_other(kind, origin).wait_recv()

    def shrink_part(i):
        arrive(i)
        for t in (i, i + DOWN_PARTS):
            token_own(t).wait()
            for e in range(1, PLANE):
                token_copy(t, e, (q + PLANE - e) % PLANE).wait_recv()

        def shrink_origin(o, carry):
            total = sums[o]
            for t in (i, i + DOWN_PARTS):
                k = slice(t * step, (t + 1) * step)
                x = rows[:, :, k].reshape(total_rows, step)
                total += jnp.dot(x, down[o, k, :], preferred_element_type=jnp.float32)
            sums[o] = total
            return carry

        lax.fori_loop(0, LINE, shrink_origin, 0)

    def mask_all():
        tag = tags[...].reshape(total_rows, lanes).astype(jnp.int32)
        tag = tag - lax.broadcasted_iota(jnp.int32, (total_rows, lanes), 1) // ADAPTER_RANK
        for o in range(LINE):
            kept = jnp.where(tag == o * (lanes // ADAPTER_RANK), sums[o], 0.0)
            shrink[o] = kept.astype(jnp.bfloat16)

    def expand(t):
        first, count = tiles[t]
        tile = 512

        def up_step(i, carry):
            c = pl.ds(pl.multiple_of(first + i * tile, tile), tile)
            total = jnp.zeros((total_rows, tile), jnp.float32)
            for o in range(LINE):
                total += jnp.dot(shrink[o], up[o, :, c], preferred_element_type=jnp.float32)
            result[:, :, c] = total.astype(jnp.bfloat16).reshape(PLANE, slots, tile)
            return carry

        lax.fori_loop(0, count // tile, up_step, 0)
        for e in range(1, PLANE):
            back(t, e, q).start()
        keep_own(t).start()

    sums[...] = jnp.zeros_like(sums)
    pass_on(0)
    for kind in range(DOWN_PARTS):
        pass_on(kind + 1)
        shrink_part(kind)
    for copy in own[2:]:
        copy.wait()
    for e in range(1, PLANE):
        tag_copy(e, (q + PLANE - e) % PLANE).wait_recv()
    mask_all()
    for t in range(len(tiles)):
        if t + 1 < len(tiles):
            pass_on(DOWN_PARTS + t + 1)
        arrive(DOWN_PARTS + t)
        expand(t)

    for e in range(1, PLANE):
        tag_copy(e, q).wait_send()
        for t in range(2 * DOWN_PARTS):
            token_copy(t, e, q).wait_send()
    for kind in range(kinds):
        for d in range(LINE):
            @pl.when((z >= d) & (z < LINE - 1))
            def _():
                to_right(kind, z - d).wait_send()

            @pl.when((z + d < LINE) & (z > 0))
            def _():
                to_left(kind, z + d).wait_send()

        for origin in origins[1:]:
            to_other(kind, origin).wait_send()
    for t in range(len(tiles)):
        keep_own(t).wait()
        for e in range(1, PLANE):
            back(t, e, q).wait_send()
            back(t, e, (q + PLANE - e) % PLANE).wait_recv()


def exchange_planes(
    tokens, down_weight, up_weight, slot_adapter_index, slot_token_length, adapter_block_table
):
    devices = lax.axis_size("adapter")
    tok_count, width = tokens.shape
    cap = 3 * tok_count // devices // 2
    lanes = down_weight.shape[1]
    loaded_block = lanes // ADAPTER_RANK
    me = lax.axis_index("adapter")
    z = me // PLANE
    _, block = route(slot_adapter_index, slot_token_length, adapter_block_table, tok_count, 0)
    owner = block // loaded_block
    rank = rank_among(owner)
    origin = owner // PLANE
    near = z + 1 - 2 * (z % 2)
    third = 2 - z // 2
    base = jnp.where(
        origin == z,
        0,
        jnp.where(origin == near, cap, jnp.where(origin == third, 2 * cap, 3 * cap + 8)),
    )
    base = jnp.where(rank < cap, base, 3 * cap + 8)
    slots = 5 * cap + 8
    slot_of_token = (owner % PLANE) * slots + base + rank
    slot_index = jnp.arange(PLANE * slots, dtype=jnp.int32)
    hit = slot_index[:, None] == slot_of_token[None, :]
    pick = hit.astype(jnp.bfloat16)
    tag = jnp.sum(jnp.where(hit, (origin * loaded_block + block % loaded_block)[None, :], 0), axis=1)
    tag = jnp.broadcast_to(tag.astype(jnp.bfloat16)[:, None], (PLANE * slots, lanes))
    tag = tag.reshape(PLANE, slots, lanes)
    dma = pltpu.SemaphoreType.DMA
    eighth = width // 8
    tiles = [(0, eighth), (eighth, eighth)] + [(i * eighth, 2 * eighth) for i in (2, 4, 6)]
    kinds = DOWN_PARTS + len(tiles)
    returned = pl.pallas_call(
        lambda *refs: plane_kernel(tiles, *refs),
        out_shape=jax.ShapeDtypeStruct((PLANE, slots, width), jnp.bfloat16),
        in_specs=[pl.BlockSpec(memory_space=pltpu.VMEM)] * 2
        + [pl.BlockSpec(memory_space=pl.ANY)] * 3,
        out_specs=pl.BlockSpec(memory_space=pl.ANY),
        scratch_shapes=[
            pltpu.VMEM((PLANE, slots, width), jnp.bfloat16),
            pltpu.VMEM((PLANE, slots, width), jnp.bfloat16),
            pltpu.VMEM((PLANE, slots, lanes), jnp.bfloat16),
            pltpu.VMEM((LINE, width, lanes), jnp.bfloat16),
            pltpu.VMEM((LINE, lanes, width), jnp.bfloat16),
            pltpu.VMEM((PLANE, slots, width), jnp.bfloat16),
            pltpu.VMEM((LINE, PLANE * slots, lanes), jnp.float32),
            pltpu.VMEM((LINE, PLANE * slots, lanes), jnp.bfloat16),
            dma((3,)),
            dma((2 * DOWN_PARTS,)),
            dma((2 * DOWN_PARTS, PLANE)),
            dma((2 * DOWN_PARTS, PLANE)),
            dma((PLANE,)),
            dma((PLANE,)),
            dma((LINE, kinds)),
            dma((LINE, kinds)),
            dma((LINE, kinds)),
            dma((LINE, kinds)),
            dma((LINE, kinds)),
            dma((len(tiles), PLANE)),
            dma((len(tiles), PLANE)),
            dma((len(tiles),)),
        ],
        compiler_params=pltpu.CompilerParams(
            collective_id=0, has_side_effects=True, vmem_limit_bytes=56 * 2**20
        ),
        cost_estimate=pl.CostEstimate(
            flops=8 * PLANE * slots * width * lanes,
            bytes_accessed=8 * PLANE * slots * width,
            transcendentals=0,
        ),
    )(tokens, pick, tag, down_weight, up_weight)
    returned = returned.reshape(PLANE * slots, width)
    update = jnp.dot(pick.T, returned, preferred_element_type=jnp.float32)
    return update.astype(jnp.bfloat16)


def solution(mesh):
    sizes = dict(mesh.shape)
    planes = sizes["groups"] == 2 and sizes["adapter"] == PLANE * LINE
    on_device = exchange_planes if planes else exchange_all
    in_specs = (
        P(("groups", "adapter"), None),
        P(None, "adapter"),
        P("adapter", None),
        P(("groups", "adapter")),
        P(("groups", "adapter")),
        P("groups"),
    )
    out_specs = P(("groups", "adapter"), None)
    return jax.shard_map(
        on_device, mesh=mesh, in_specs=in_specs, out_specs=out_specs, check_vma=False
    )
```
